32 devices in a mesh: groups: 2 (over y), expert: 4 (over z), dp: 4 (over x, core).
Axes of the slice: x: 2, y: 2, z: 4, core: 2. Of those that a mesh axis runs over, the one named last changes fastest.
Arguments:
- tokens: bfloat16 [4096, 1024], P(('groups', 'expert', 'dp')), parts along dimension 0, may hold values from -6 to 6
- expert_ids: int32 [4096, 8], P(('groups', 'expert', 'dp')), parts along dimension 0, may hold values from 0 to 63, all different within a row; in each aligned block of 128 rows (0 to 127, 128 to 255, ...) at most 16 rows name the same one
- gate_values: float32 [4096, 8], P(('groups', 'expert', 'dp')), parts along dimension 0, may hold values from 0.1 to 1
- w_gate_up: bfloat16 [64, 1024, 768], P('expert', 'dp'), may hold values from -0.1875 to 0.1875
- w_down: bfloat16 [64, 384, 1024], P('expert', None, 'dp'), may hold values from -0.3125 to 0.3125
- new_slot: int32 [64], replicated, may hold values from 0 to 63, each once
- cotangent: bfloat16 [4096, 1024], P(('groups', 'expert', 'dp')), parts along dimension 0, may hold values from -6 to 6
Outputs:
- layer_out: bfloat16 [4096, 1024], P(('groups', 'expert', 'dp')), parts along dimension 0
- d_tokens: bfloat16 [4096, 1024], P(('groups', 'expert', 'dp')), parts along dimension 0
- d_gate_up: bfloat16 [128, 1024, 768], P(('groups', 'expert'), 'dp'), parts along dimension 0
- d_down: bfloat16 [128, 384, 1024], P(('groups', 'expert'), None, 'dp'), parts along dimension 0
The draws below stay inside these ranges and needn't reach their ends.
There are 2 independent parts, one for each index of `groups`. The reference program is written for one: setup_inputs(seed, part) draws one part's arguments, and reference() takes and returns one part's arrays. A program takes and returns all parts, laid end to end along the dimension named above; an argument that names none is the same for every part. Nothing has to cross between parts.
Inputs may be any that keep to these rules, and one draw needn't show every extreme that they name: `expert_ids`: each row names 8 different experts; among the 128 rows of one device no expert is named by more than 16 rows, and on some devices some expert is named by exactly 16. `new_slot`: every number appears once, so each slot holds one expert; slot s belongs to index s // (64 / 4) of axis expert.
All inputs are finite; a program needn't handle non-finite values.
Results may differ from the reference program's by a relative error of at most 0.0095.
Values may be sent and summed in bfloat16 or wider, within the bound.
A program may use at most 192 MiB of HBM per device.

```python
import math
from functools import partial
import jax
import jax.numpy as jnp
import numpy as np
from jax import lax

D = 1024
FF = 384
EXPERTS = 64
TOP = 8
TOK_DEV = 128
MOST = 16
TOKENS = 2048
N_EXPERT = 4
N_DP = 4


def block_levels(stream_key, shape, pieces, low, high):
    level = 1.0
    for axis_at, shards_of in pieces:
        steps = jax.random.uniform(jax.random.fold_in(jax.random.fold_in(stream_key, 6), axis_at), (shards_of,), jnp.float32, low / len(pieces), high / len(pieces))
        level = level * jnp.repeat(jnp.exp(steps), shape[axis_at] // shards_of).reshape((-1,) + (1,) * (len(shape) - 1 - axis_at))
    return level


def shared_out(key, own, number, rows, count, top, limit, slope):
    ranking = jax.random.permutation(key, count)
    packed, ordinary = portions_of(count, rows * top, limit, slope, True), portions_of(count, rows * top, limit, slope, False)
    places = jnp.arange(count)

    def named(sizes, rotation):
        used = int((sizes > 0).sum())
        fixed = max(1, used // 4)
        passed = fixed + (places - fixed + rotation * (used - fixed)) % max(1, count - fixed)
        return jnp.zeros((count,), jnp.int32).at[ranking[jnp.where(places < fixed, places, passed)]].set(jnp.asarray(sizes, jnp.int32))

    sizes = jnp.where(number % 4 == 0, named(packed, number // 4), named(ordinary, number - number // 4 - 1))
    mixed = jax.random.permutation(jax.random.fold_in(own, 3), count)
    giver, receiver = mixed[0:count // 2 * 2:2], mixed[1:count // 2 * 2:2]
    slack = jnp.minimum(sizes[giver] - 1, limit - sizes[receiver]) // 2
    slack = jnp.where((giver == ranking[0]) | (receiver == ranking[0]) | (sizes[receiver] == 0), 0, jnp.maximum(slack, 0))
    passed = jax.random.randint(jax.random.fold_in(own, 4), (count // 2,), 0, 1 << 20) % (slack + 1)
    sizes = sizes.at[giver].add(-passed).at[receiver].add(passed)
    items = jnp.searchsorted(jnp.cumsum(sizes), jnp.arange(rows * top), side="right").astype(jnp.int32)
    grid = items.reshape(top, rows).T
    grid = grid[jax.random.permutation(jax.random.fold_in(own, 1), rows)]
    rotation = jax.random.randint(jax.random.fold_in(own, 2), (rows, 1), 0, top)
    return jnp.take_along_axis(grid, (jnp.arange(top)[None, :] + rotation) % top, axis=1)


def portions_of(amount, total, bound, skew, full):
    portions = [(1 << 20) // math.isqrt(standing ** skew) + 1 for standing in range(1, amount + 1)]
    largest = bound if full else min(bound, max(-(-total // amount), total * portions[0] // sum(portions)))
    least = 1 if total - largest >= amount - 1 else 0
    holding, spare = [largest] + [least] * (amount - 1), total - largest - least * (amount - 1)
    while spare > 0:
        movable = [i for i in range(1, amount) if holding[i] < largest] or [i for i in range(1, amount) if holding[i] < bound]
        mass, remaining = sum([portions[i] for i in movable]), spare
        for i in movable:
            extra = min(bound - holding[i], max(1, remaining * portions[i] // mass), spare)
            holding[i] = holding[i] + extra
            spare = spare - extra
    return np.array(holding)


def normal_values(stream_key, extent, scale, bound, shards=(), held_as=jnp.bfloat16):
    result = scale * jax.random.normal(stream_key, extent, jnp.float32)
    if shards:
        result = result * block_levels(stream_key, extent, shards, -0.22, 0.18)
    return jnp.clip(result, -bound, bound).astype(held_as)


def setup_inputs(seed: int = 0, part: int = 0) -> dict:
    arg_keys = jax.random.split(jax.random.key(seed), 8)
    own_keys = jax.random.split(jax.random.fold_in(arg_keys[7], part), 8)
    tokens = normal_values(own_keys[0], (TOKENS, D), 1.0, 6.0, ((0, 16),))
    expert_ids_keys = jax.random.split(jax.random.fold_in(own_keys[1], 1), TOKENS // TOK_DEV)
    expert_ids_turns = jax.random.permutation(jax.random.fold_in(own_keys[1], 3), TOKENS // TOK_DEV)
    expert_ids = jax.vmap(lambda own, number: shared_out(jax.random.fold_in(own_keys[1], 2), own, number, TOK_DEV, EXPERTS, TOP, MOST, 2))(expert_ids_keys, expert_ids_turns).reshape((TOKENS, TOP))
    gate_values = jnp.clip(0.1 + 0.9 * jax.random.uniform(own_keys[2], (TOKENS, TOP), jnp.float32) ** block_levels(own_keys[2], (TOKENS, TOP), ((0, 16),), -0.2, 0.2), 0.1, 1.0)
    w_gate_up = normal_values(arg_keys[3], (EXPERTS, D, 2 * FF), D ** -0.5, 0.1875, ((0, 4), (1, 4)))
    w_down = normal_values(arg_keys[4], (EXPERTS, FF, D), FF ** -0.5, 0.3125, ((0, 4), (2, 4)))
    new_slot = jax.random.permutation(arg_keys[5], EXPERTS).astype(jnp.int32)
    cotangent = normal_values(own_keys[6], (TOKENS, D), 1.0, 6.0, ((0, 16),))
    return dict(tokens=tokens, expert_ids=expert_ids, gate_values=gate_values, w_gate_up=w_gate_up, w_down=w_down, new_slot=new_slot, cotangent=cotangent)


def route_table(expert_ids):
    flat_ids = expert_ids.reshape(-1)
    matches = flat_ids[:, None] == jnp.arange(EXPERTS, dtype=jnp.int32)[None, :]
    indicator = matches.astype(jnp.int32)
    earlier = jnp.cumsum(indicator, axis=0) - indicator
    position = jnp.sum(jnp.where(matches, earlier, 0), axis=1).astype(jnp.int32)
    target_cell = (flat_ids * MOST + position).astype(jnp.int32)
    entries = flat_ids.shape[0]
    table = jnp.full((EXPERTS * MOST,), entries, jnp.int32).at[target_cell].set(jnp.arange(entries, dtype=jnp.int32))
    return table.reshape(EXPERTS, MOST)


def expert_step(padded_tokens, padded_cot, carry, inputs):
    out_sum, grad_sum = carry
    rows_index, gate_cells, weight_gu, weight_dn = inputs
    flat_index = rows_index.reshape(-1)
    gate_flat = gate_cells.reshape(-1)
    arrived = padded_tokens[flat_index]
    cot_rows = padded_cot[flat_index]
    gate_up = jnp.dot(arrived, weight_gu, preferred_element_type=jnp.float32)
    gate_part = gate_up[:, :FF]
    up_part = gate_up[:, FF:]
    sigmoid_g = jax.nn.sigmoid(gate_part)
    silu_g = gate_part * sigmoid_g
    activation = (silu_g * up_part).astype(jnp.bfloat16)
    expert_out = jnp.dot(activation, weight_dn, preferred_element_type=jnp.float32).astype(jnp.bfloat16)
    out_sum = out_sum.at[flat_index].add(gate_flat[:, None] * expert_out.astype(jnp.float32))
    d_outputs = (gate_flat[:, None] * cot_rows.astype(jnp.float32)).astype(jnp.bfloat16)
    d_act = jnp.dot(d_outputs, weight_dn.T, preferred_element_type=jnp.float32)
    d_gate = d_act * up_part * sigmoid_g * (1.0 + gate_part * (1.0 - sigmoid_g))
    d_up = d_act * silu_g
    d_gate_up = jnp.concatenate([d_gate, d_up], axis=1).astype(jnp.bfloat16)
    d_rows = jnp.dot(d_gate_up, weight_gu.T, preferred_element_type=jnp.float32).astype(jnp.bfloat16)
    grad_sum = grad_sum.at[flat_index].add(d_rows.astype(jnp.float32))
    x_four = arrived.reshape(N_EXPERT, N_DP, MOST, D).astype(jnp.float32)
    g_four = d_gate_up.reshape(N_EXPERT, N_DP, MOST, 2 * FF).astype(jnp.float32)
    a_four = activation.reshape(N_EXPERT, N_DP, MOST, FF).astype(jnp.float32)
    o_four = d_outputs.reshape(N_EXPERT, N_DP, MOST, D).astype(jnp.float32)
    part_gu = jnp.einsum("ijmd,ijmf->jdf", x_four, g_four)
    part_dn = jnp.einsum("ijmf,ijmd->jfd", a_four, o_four)
    rounded_gu = lax.optimization_barrier(part_gu.astype(jnp.bfloat16))
    rounded_dn = lax.optimization_barrier(part_dn.astype(jnp.bfloat16))
    grad_gu = jnp.sum(rounded_gu.astype(jnp.float32), axis=0).astype(jnp.bfloat16)
    grad_dn = jnp.sum(rounded_dn.astype(jnp.float32), axis=0).astype(jnp.bfloat16)
    return (out_sum, grad_sum), (grad_gu, grad_dn)


def reference(tokens, expert_ids, gate_values, w_gate_up, w_down, new_slot, cotangent):
    devices = N_EXPERT * N_DP
    entries = TOK_DEV * TOP
    tables = jax.vmap(route_table)(expert_ids.reshape(devices, TOK_DEV, TOP))
    valid = tables < entries
    device_base = (jnp.arange(devices, dtype=jnp.int32) * TOK_DEV)[:, None, None]
    row_index = jnp.where(valid, device_base + tables // TOP, TOKENS).astype(jnp.int32)
    gate_flat = gate_values.reshape(devices, entries)
    clipped = jnp.minimum(tables, entries - 1).reshape(devices, -1).astype(jnp.int32)
    picked = jnp.take_along_axis(gate_flat, clipped, axis=1).reshape(tables.shape)
    gate_cells = jnp.where(valid, picked, jnp.zeros_like(picked))
    blank_row = jnp.zeros((1, D), tokens.dtype)
    padded_tokens = jnp.concatenate([tokens, blank_row], axis=0)
    padded_cot = jnp.concatenate([cotangent, blank_row], axis=0)
    inputs = (jnp.swapaxes(row_index, 0, 1), jnp.swapaxes(gate_cells, 0, 1), w_gate_up, w_down)
    start = (jnp.zeros((TOKENS + 1, D), jnp.float32), jnp.zeros((TOKENS + 1, D), jnp.float32))
    stepper = partial(expert_step, padded_tokens, padded_cot)
    (out_sum, grad_sum), (grads_gu, grads_dn) = lax.scan(stepper, start, inputs)
    layer_out = out_sum[:TOKENS].astype(jnp.bfloat16)
    d_tokens = grad_sum[:TOKENS].astype(jnp.bfloat16)
    d_gate_up = jnp.zeros_like(grads_gu).at[new_slot].set(grads_gu)
    d_down = jnp.zeros_like(grads_dn).at[new_slot].set(grads_dn)
    return (layer_out, d_tokens, d_gate_up, d_down)
```

```python
import jax
import jax.numpy as jnp
from jax import lax
from jax.sharding import PartitionSpec as P

MOST = 16


def relocate(gate_up, down, inverse):
    expert_peers = lax.axis_size("expert")
    home_slots = gate_up.shape[0]
    spread_gu = gate_up.reshape(
        home_slots, expert_peers, gate_up.shape[1] // expert_peers, gate_up.shape[2]
    )
    spread_dn = down.reshape(home_slots, expert_peers, down.shape[1] // expert_peers, down.shape[2])
    got_gu, got_dn = (
        lax.all_to_all(spread_gu, "expert", split_axis=1, concat_axis=0, tiled=True),
        lax.all_to_all(spread_dn, "expert", split_axis=1, concat_axis=0, tiled=True),
    )
    experts = home_slots * expert_peers
    slot_order = inverse.reshape(expert_peers, home_slots).T
    pick_gu = got_gu.reshape(experts, got_gu.shape[2], got_gu.shape[3])[slot_order]
    pick_dn = got_dn.reshape(experts, got_dn.shape[2], got_dn.shape[3])[slot_order]
    new_gu, new_dn = (
        lax.all_to_all(pick_gu, "expert", split_axis=1, concat_axis=1, tiled=True),
        lax.all_to_all(pick_dn, "expert", split_axis=1, concat_axis=1, tiled=True),
    )
    return (new_gu.reshape(gate_up.shape), new_dn.reshape(down.shape))


def route_cells(expert_ids, slot_map):
    experts = slot_map.shape[0]
    flat_ids = expert_ids.reshape(-1)
    matches = flat_ids[:, None] == jnp.arange(experts, dtype=jnp.int32)[None, :]
    indicator = matches.astype(jnp.int32)
    earlier = jnp.cumsum(indicator, axis=0) - indicator
    position = jnp.sum(jnp.where(matches, earlier, 0), axis=1)
    target = jnp.sum(jnp.where(matches, slot_map[None, :], 0), axis=1)
    target_cell = target * MOST + position
    entries = flat_ids.shape[0]
    source = (
        jnp.full((experts * MOST,), entries, jnp.int32)
        .at[target_cell]
        .set(jnp.arange(entries, dtype=jnp.int32))
    )
    return (target_cell, source)


def routed_shards(tokens, expert_ids, gate_values, w_gate_up, w_down, new_slot, cotangent):
    expert_peers = lax.axis_size("expert")
    home_slots = w_gate_up.shape[0]
    model_width = tokens.shape[1]
    hidden_width = w_down.shape[1]
    top_count = expert_ids.shape[1]
    token_count = tokens.shape[0]
    inverse = jnp.argsort(new_slot)
    local_gu, local_dn = relocate(w_gate_up, w_down, inverse)
    full_gu, full_dn = (
        lax.all_gather(local_gu, "dp", axis=1, tiled=True),
        lax.all_gather(local_dn, "dp", axis=2, tiled=True),
    )
    target_cell, source = route_cells(expert_ids, new_slot)
    blank_row = jnp.zeros((1, model_width), jnp.bfloat16)
    token_row = source // top_count
    cell_gates = jnp.concatenate([gate_values.reshape(-1), jnp.zeros((1,), jnp.float32)])[source]
    outgoing = jnp.concatenate([tokens, blank_row], axis=0)[token_row]
    cot_rows = jnp.concatenate([cotangent, blank_row], axis=0)[token_row]
    scaled_cot = (cell_gates[:, None] * cot_rows.astype(jnp.float32)).astype(jnp.bfloat16)
    row_shape = (expert_peers, home_slots, MOST, model_width)
    arrived = lax.all_to_all(
        outgoing.reshape(row_shape), "expert", split_axis=0, concat_axis=0, tiled=True
    )
    gate_up = jnp.einsum("shmd,hdf->shmf", arrived, full_gu, preferred_element_type=jnp.float32)
    gate_part = gate_up[..., :hidden_width]
    up_part = gate_up[..., hidden_width:]
    sigmoid_g = jax.nn.sigmoid(gate_part)
    silu_g = gate_part * sigmoid_g
    activation = (silu_g * up_part).astype(jnp.bfloat16)
    expert_out = jnp.einsum(
        "shmf,hfd->shmd", activation, full_dn, preferred_element_type=jnp.float32
    ).astype(jnp.bfloat16)
    returned = lax.all_to_all(expert_out, "expert", split_axis=0, concat_axis=0, tiled=True)
    gathered_out = returned.reshape(-1, model_width)[target_cell].reshape(
        token_count, top_count, model_width
    )
    layer_out = jnp.sum(gate_values[:, :, None] * gathered_out.astype(jnp.float32), axis=1).astype(
        jnp.bfloat16
    )
    d_outputs = lax.all_to_all(
        scaled_cot.reshape(row_shape), "expert", split_axis=0, concat_axis=0, tiled=True
    )
    d_act = jnp.einsum("shmd,hfd->shmf", d_outputs, full_dn, preferred_element_type=jnp.float32)
    d_gate = d_act * up_part * sigmoid_g * (1.0 + gate_part * (1.0 - sigmoid_g))
    d_up = d_act * silu_g
    d_gate_up = jnp.concatenate([d_gate, d_up], axis=-1).astype(jnp.bfloat16)
    d_rows = jnp.einsum(
        "shmf,hdf->shmd", d_gate_up, full_gu, preferred_element_type=jnp.float32
    ).astype(jnp.bfloat16)
    rows_back = lax.all_to_all(d_rows, "expert", split_axis=0, concat_axis=0, tiled=True)
    gathered_grads = rows_back.reshape(-1, model_width)[target_cell].reshape(
        token_count, top_count, model_width
    )
    d_tokens = jnp.sum(gathered_grads.astype(jnp.float32), axis=1).astype(jnp.bfloat16)
    part_gu = jnp.einsum("shmd,shmf->hdf", arrived, d_gate_up, preferred_element_type=jnp.float32)
    part_dn = jnp.einsum(
        "shmd,shmf->hdf", d_outputs, activation, preferred_element_type=jnp.float32
    )
    sum_gu, sum_dn = (
        lax.psum_scatter(
            part_gu.astype(jnp.bfloat16), "dp", scatter_dimension=1, tiled=True
        ).astype(jnp.float32),
        lax.psum_scatter(
            part_dn.astype(jnp.bfloat16), "dp", scatter_dimension=1, tiled=True
        ).astype(jnp.float32),
    )
    grad_gu = sum_gu.astype(jnp.bfloat16)
    grad_dn = jnp.swapaxes(sum_dn, 1, 2).astype(jnp.bfloat16)
    return (layer_out, d_tokens, grad_gu, grad_dn)


def cell_select(ids, gates, experts_here):
    match = ids[..., None] == experts_here
    member = jnp.any(match, axis=-2)
    gate = jnp.sum(jnp.where(match, gates[..., None], 0.0), axis=-2)
    count = ids.shape[-2]
    below = (jnp.arange(count)[:, None] > jnp.arange(count)[None, :]).astype(jnp.bfloat16)
    rank = jnp.einsum(
        "tu,...uh->...th",
        below,
        member.astype(jnp.bfloat16),
        preferred_element_type=jnp.float32,
    ).astype(jnp.int32)
    rank = jnp.where(member, rank, -1)
    rank = jnp.swapaxes(rank, -1, -2)
    gate = jnp.swapaxes(gate, -1, -2)
    select = rank[..., None, :] == jnp.arange(MOST, dtype=jnp.int32)[:, None]
    cell_gate = jnp.sum(jnp.where(select, gate[..., None, :], 0.0), axis=-1)
    return select, cell_gate


def pick_rows(spec, select, rows):
    return jnp.einsum(
        spec, select.astype(jnp.bfloat16), rows, preferred_element_type=jnp.float32
    )


def shared_shards(tokens, expert_ids, gate_values, w_gate_up, w_down, new_slot, cotangent):
    expert_peers = lax.axis_size("expert")
    dp_peers = lax.axis_size("dp")
    me = lax.axis_index("expert")
    home_slots = w_gate_up.shape[0]
    model_width = tokens.shape[1]
    hidden_width = w_down.shape[1]
    token_count = tokens.shape[0]
    share = model_width // dp_peers
    here = me * home_slots + jnp.arange(home_slots, dtype=jnp.int32)

    both = jnp.concatenate([tokens, cotangent], axis=1)
    rows_all = lax.all_gather(both, "expert", axis=0, tiled=False)
    ids_all = lax.all_gather(expert_ids, "expert", axis=0, tiled=False)
    gates_all = lax.all_gather(gate_values, "expert", axis=0, tiled=False)
    full_gu = lax.all_gather(w_gate_up, "dp", axis=1, tiled=True)
    full_dn = lax.all_gather(w_down, "dp", axis=2, tiled=True)

    select, cell_gate = cell_select(ids_all, gates_all, here)
    cell_rows = pick_rows("shmt,std->hsmd", select, rows_all)
    cell_gate = jnp.swapaxes(cell_gate, 0, 1)
    cell_count = expert_peers * MOST
    arrived = cell_rows[..., :model_width].astype(jnp.bfloat16)
    arrived = arrived.reshape(home_slots, cell_count, model_width)
    d_outputs = (cell_gate[..., None] * cell_rows[..., model_width:]).astype(jnp.bfloat16)
    d_outputs = d_outputs.reshape(home_slots, cell_count, model_width)

    gate_up = jnp.einsum("hrd,hdf->hrf", arrived, full_gu, preferred_element_type=jnp.float32)
    d_act = jnp.einsum("hrd,hfd->hrf", d_outputs, full_dn, preferred_element_type=jnp.float32)
    gate_part = gate_up[..., :hidden_width]
    up_part = gate_up[..., hidden_width:]
    sigmoid_g = jax.nn.sigmoid(gate_part)
    silu_g = gate_part * sigmoid_g
    activation = (silu_g * up_part).astype(jnp.bfloat16)
    d_gate = d_act * up_part * sigmoid_g * (1.0 + gate_part * (1.0 - sigmoid_g))
    d_up = d_act * silu_g
    payload = jnp.concatenate(
        [d_gate.astype(jnp.bfloat16), d_up.astype(jnp.bfloat16), activation], axis=-1
    )
    payload_all = lax.all_gather(payload, "expert", axis=0, tiled=True)

    d_gate_up = payload[..., : 2 * hidden_width]
    expert_out = jnp.einsum(
        "hrf,hfd->hrd", activation, full_dn, preferred_element_type=jnp.float32
    ).astype(jnp.bfloat16)
    d_rows = jnp.einsum(
        "hrf,hdf->hrd", d_gate_up, full_gu, preferred_element_type=jnp.float32
    ).astype(jnp.bfloat16)
    cells = (home_slots, expert_peers, MOST, model_width)
    scaled_out = cell_gate[..., None] * expert_out.reshape(cells).astype(jnp.float32)
    part_out = jnp.einsum(
        "shmt,hsmd->std",
        select.astype(jnp.float32),
        scaled_out,
        precision=lax.Precision.HIGHEST,
        preferred_element_type=jnp.float32,
    ).astype(jnp.bfloat16)
    part_grad = pick_rows("shmt,hsmd->std", select, d_rows.reshape(cells)).astype(jnp.bfloat16)
    back = lax.all_to_all(
        jnp.concatenate([part_out, part_grad], axis=-1),
        "expert",
        split_axis=0,
        concat_axis=0,
        tiled=True,
    )
    summed = jnp.sum(back.astype(jnp.float32), axis=0).astype(jnp.bfloat16)
    layer_out = summed[:, :model_width]
    d_tokens = summed[:, model_width:]

    wide = rows_all.reshape(expert_peers, token_count, 2, dp_peers, share)
    wide = jnp.transpose(wide, (3, 0, 1, 2, 4))
    narrow = lax.all_to_all(wide, "dp", split_axis=0, concat_axis=0, tiled=True)
    narrow = narrow.reshape(dp_peers, expert_peers, token_count, 2 * share)
    ids_group = lax.all_gather(ids_all, "dp", axis=0, tiled=False)
    gates_group = lax.all_gather(gates_all, "dp", axis=0, tiled=False)
    inverse = jnp.argsort(new_slot).astype(jnp.int32)
    mine = lax.dynamic_slice_in_dim(inverse, me * home_slots, home_slots)
    select_new, gate_new = cell_select(ids_group, gates_group, mine)
    new_rows = pick_rows("pshmt,pstc->hpsmc", select_new, narrow)
    gate_new = jnp.transpose(gate_new, (2, 0, 1, 3))
    group_rows = dp_peers * cell_count
    new_tokens = new_rows[..., :share].astype(jnp.bfloat16)
    new_tokens = new_tokens.reshape(home_slots, group_rows, share)
    new_douts = (gate_new[..., None] * new_rows[..., share:]).astype(jnp.bfloat16)
    new_douts = new_douts.reshape(home_slots, group_rows, share)

    mine_rows = payload_all[mine]
    group_payload = lax.all_gather(mine_rows, "dp", axis=1, tiled=True)
    grad_gu = jnp.einsum(
        "hrc,hrf->hcf",
        new_tokens,
        group_payload[..., : 2 * hidden_width],
        preferred_element_type=jnp.float32,
    ).astype(jnp.bfloat16)
    grad_dn = jnp.einsum(
        "hrf,hrc->hfc",
        group_payload[..., 2 * hidden_width :],
        new_douts,
        preferred_element_type=jnp.float32,
    ).astype(jnp.bfloat16)
    return (layer_out, d_tokens, grad_gu, grad_dn)


def shards(tokens, expert_ids, *rest):
    if lax.axis_size("expert") < expert_ids.shape[1]:
        return shared_shards(tokens, expert_ids, *rest)
    return routed_shards(tokens, expert_ids, *rest)


def solution(mesh):
    return jax.shard_map(
        shards,
        mesh=mesh,
        in_specs=(
            P(("groups", "expert", "dp"), None),
            P(("groups", "expert", "dp"), None),
            P(("groups", "expert", "dp"), None),
            P("expert", "dp", None),
            P("expert", None, "dp"),
            P(),
            P(("groups", "expert", "dp"), None),
        ),
        out_specs=(
            P(("groups", "expert", "dp"), None),
            P(("groups", "expert", "dp"), None),
            P(("groups", "expert"), "dp", None),
            P(("groups", "expert"), None, "dp"),
        ),
        check_vma=False,
    )
```

```python
import jax
import jax.numpy as jnp
from jax import lax
from jax.sharding import PartitionSpec as P

MOST = 16


def relocate(gate_up, down, inverse):
    expert_peers = lax.axis_size("expert")
    home_slots = gate_up.shape[0]
    spread_gu = gate_up.reshape(
        home_slots, expert_peers, gate_up.shape[1] // expert_peers, gate_up.shape[2]
    )
    spread_dn = down.reshape(home_slots, expert_peers, down.shape[1] // expert_peers, down.shape[2])
    got_gu, got_dn = (
        lax.all_to_all(spread_gu, "expert", split_axis=1, concat_axis=0, tiled=True),
        lax.all_to_all(spread_dn, "expert", split_axis=1, concat_axis=0, tiled=True),
    )
    experts = home_slots * expert_peers
    slot_order = inverse.reshape(expert_peers, home_slots).T
    pick_gu = got_gu.reshape(experts, got_gu.shape[2], got_gu.shape[3])[slot_order]
    pick_dn = got_dn.reshape(experts, got_dn.shape[2], got_dn.shape[3])[slot_order]
    new_gu, new_dn = (
        lax.all_to_all(pick_gu, "expert", split_axis=1, concat_axis=1, tiled=True),
        lax.all_to_all(pick_dn, "expert", split_axis=1, concat_axis=1, tiled=True),
    )
    return (new_gu.reshape(gate_up.shape), new_dn.reshape(down.shape))


def route_cells(expert_ids, slot_map):
    experts = slot_map.shape[0]
    flat_ids = expert_ids.reshape(-1)
    matches = flat_ids[:, None] == jnp.arange(experts, dtype=jnp.int32)[None, :]
    indicator = matches.astype(jnp.int32)
    earlier = jnp.cumsum(indicator, axis=0) - indicator
    position = jnp.sum(jnp.where(matches, earlier, 0), axis=1)
    target = jnp.sum(jnp.where(matches, slot_map[None, :], 0), axis=1)
    target_cell = target * MOST + position
    entries = flat_ids.shape[0]
    source = (
        jnp.full((experts * MOST,), entries, jnp.int32)
        .at[target_cell]
        .set(jnp.arange(entries, dtype=jnp.int32))
    )
    return (target_cell, source)


def routed_shards(tokens, expert_ids, gate_values, w_gate_up, w_down, new_slot, cotangent):
    expert_peers = lax.axis_size("expert")
    home_slots = w_gate_up.shape[0]
    model_width = tokens.shape[1]
    hidden_width = w_down.shape[1]
    top_count = expert_ids.shape[1]
    token_count = tokens.shape[0]
    inverse = jnp.argsort(new_slot)
    local_gu, local_dn = relocate(w_gate_up, w_down, inverse)
    full_gu, full_dn = (
        lax.all_gather(local_gu, "dp", axis=1, tiled=True),
        lax.all_gather(local_dn, "dp", axis=2, tiled=True),
    )
    target_cell, source = route_cells(expert_ids, new_slot)
    blank_row = jnp.zeros((1, model_width), jnp.bfloat16)
    token_row = source // top_count
    cell_gates = jnp.concatenate([gate_values.reshape(-1), jnp.zeros((1,), jnp.float32)])[source]
    outgoing = jnp.concatenate([tokens, blank_row], axis=0)[token_row]
    cot_rows = jnp.concatenate([cotangent, blank_row], axis=0)[token_row]
    scaled_cot = (cell_gates[:, None] * cot_rows.astype(jnp.float32)).astype(jnp.bfloat16)
    row_shape = (expert_peers, home_slots, MOST, model_width)
    arrived = lax.all_to_all(
        outgoing.reshape(row_shape), "expert", split_axis=0, concat_axis=0, tiled=True
    )
    gate_up = jnp.einsum("shmd,hdf->shmf", arrived, full_gu, preferred_element_type=jnp.float32)
    gate_part = gate_up[..., :hidden_width]
    up_part = gate_up[..., hidden_width:]
    sigmoid_g = jax.nn.sigmoid(gate_part)
    silu_g = gate_part * sigmoid_g
    activation = (silu_g * up_part).astype(jnp.bfloat16)
    expert_out = jnp.einsum(
        "shmf,hfd->shmd", activation, full_dn, preferred_element_type=jnp.float32
    ).astype(jnp.bfloat16)
    returned = lax.all_to_all(expert_out, "expert", split_axis=0, concat_axis=0, tiled=True)
    gathered_out = returned.reshape(-1, model_width)[target_cell].reshape(
        token_count, top_count, model_width
    )
    layer_out = jnp.sum(gate_values[:, :, None] * gathered_out.astype(jnp.float32), axis=1).astype(
        jnp.bfloat16
    )
    d_outputs = lax.all_to_all(
        scaled_cot.reshape(row_shape), "expert", split_axis=0, concat_axis=0, tiled=True
    )
    d_act = jnp.einsum("shmd,hfd->shmf", d_outputs, full_dn, preferred_element_type=jnp.float32)
    d_gate = d_act * up_part * sigmoid_g * (1.0 + gate_part * (1.0 - sigmoid_g))
    d_up = d_act * silu_g
    d_gate_up = jnp.concatenate([d_gate, d_up], axis=-1).astype(jnp.bfloat16)
    d_rows = jnp.einsum(
        "shmf,hdf->shmd", d_gate_up, full_gu, preferred_element_type=jnp.float32
    ).astype(jnp.bfloat16)
    rows_back = lax.all_to_all(d_rows, "expert", split_axis=0, concat_axis=0, tiled=True)
    gathered_grads = rows_back.reshape(-1, model_width)[target_cell].reshape(
        token_count, top_count, model_width
    )
    d_tokens = jnp.sum(gathered_grads.astype(jnp.float32), axis=1).astype(jnp.bfloat16)
    part_gu = jnp.einsum("shmd,shmf->hdf", arrived, d_gate_up, preferred_element_type=jnp.float32)
    part_dn = jnp.einsum(
        "shmd,shmf->hdf", d_outputs, activation, preferred_element_type=jnp.float32
    )
    sum_gu, sum_dn = (
        lax.psum_scatter(
            part_gu.astype(jnp.bfloat16), "dp", scatter_dimension=1, tiled=True
        ).astype(jnp.float32),
        lax.psum_scatter(
            part_dn.astype(jnp.bfloat16), "dp", scatter_dimension=1, tiled=True
        ).astype(jnp.float32),
    )
    grad_gu = sum_gu.astype(jnp.bfloat16)
    grad_dn = jnp.swapaxes(sum_dn, 1, 2).astype(jnp.bfloat16)
    return (layer_out, d_tokens, grad_gu, grad_dn)


def cell_select(ids, gates, experts_here):
    match = ids[..., None] == experts_here
    member = jnp.any(match, axis=-2)
    gate = jnp.sum(jnp.where(match, gates[..., None], 0.0), axis=-2)
    count = ids.shape[-2]
    below = (jnp.arange(count)[:, None] > jnp.arange(count)[None, :]).astype(jnp.bfloat16)
    rank = jnp.einsum(
        "tu,...uh->...th",
        below,
        member.astype(jnp.bfloat16),
        preferred_element_type=jnp.float32,
    ).astype(jnp.int32)
    rank = jnp.where(member, rank, -1)
    rank = jnp.swapaxes(rank, -1, -2)
    gate = jnp.swapaxes(gate, -1, -2)
    select = rank[..., None, :] == jnp.arange(MOST, dtype=jnp.int32)[:, None]
    cell_gate = jnp.sum(jnp.where(select, gate[..., None, :], 0.0), axis=-1)
    return select, cell_gate


def pick_rows(spec, select, rows):
    return jnp.einsum(
        spec, select.astype(jnp.bfloat16), rows, preferred_element_type=jnp.float32
    )


def shared_shards(tokens, expert_ids, gate_values, w_gate_up, w_down, new_slot, cotangent):
    expert_peers = lax.axis_size("expert")
    dp_peers = lax.axis_size("dp")
    me = lax.axis_index("expert")
    home_slots = w_gate_up.shape[0]
    model_width = tokens.shape[1]
    hidden_width = w_down.shape[1]
    token_count = tokens.shape[0]
    share = model_width // dp_peers
    here = me * home_slots + jnp.arange(home_slots, dtype=jnp.int32)

    both = jnp.concatenate([tokens, cotangent], axis=1)
    rows_all = lax.all_gather(both, "expert", axis=0, tiled=False)
    ids_all = lax.all_gather(expert_ids, "expert", axis=0, tiled=False)
    gates_all = lax.all_gather(gate_values, "expert", axis=0, tiled=False)
    full_gu = lax.all_gather(w_gate_up, "dp", axis=1, tiled=True)
    full_dn = lax.all_gather(w_down, "dp", axis=2, tiled=True)

    select, cell_gate = cell_select(ids_all, gates_all, here)
    cell_rows = pick_rows("shmt,std->hsmd", select, rows_all)
    cell_gate = jnp.swapaxes(cell_gate, 0, 1)
    cell_count = expert_peers * MOST
    arrived = cell_rows[..., :model_width].astype(jnp.bfloat16)
    arrived = arrived.reshape(home_slots, cell_count, model_width)
    d_outputs = (cell_gate[..., None] * cell_rows[..., model_width:]).astype(jnp.bfloat16)
    d_outputs = d_outputs.reshape(home_slots, cell_count, model_width)

    inverse = jnp.argsort(new_slot).astype(jnp.int32)
    wide = rows_all.reshape(expert_peers, token_count, 2, dp_peers, share)
    wide = jnp.transpose(wide, (3, 0, 1, 2, 4))
    narrow = lax.all_to_all(wide, "dp", split_axis=0, concat_axis=0, tiled=True)
    narrow = narrow.reshape(dp_peers, expert_peers, token_count, 2 * share)
    ids_group = lax.all_gather(ids_all, "dp", axis=0, tiled=False)
    gates_group = lax.all_gather(gates_all, "dp", axis=0, tiled=False)
    mine = lax.dynamic_slice_in_dim(inverse, me * home_slots, home_slots)
    select_new, gate_new = cell_select(ids_group, gates_group, mine)
    new_rows = pick_rows("pshmt,pstc->hpsmc", select_new, narrow)
    gate_new = jnp.transpose(gate_new, (2, 0, 1, 3))
    group_rows = dp_peers * cell_count
    new_tokens = new_rows[..., :share].astype(jnp.bfloat16)
    new_tokens = new_tokens.reshape(home_slots, group_rows, share)
    new_douts = (gate_new[..., None] * new_rows[..., share:]).astype(jnp.bfloat16)
    new_douts = new_douts.reshape(home_slots, group_rows, share)
    arrived, d_outputs, new_tokens, new_douts = lax.optimization_barrier(
        (arrived, d_outputs, new_tokens, new_douts)
    )

    gate_up = jnp.einsum("hrd,hdf->hrf", arrived, full_gu, preferred_element_type=jnp.float32)
    d_act = jnp.einsum("hrd,hfd->hrf", d_outputs, full_dn, preferred_element_type=jnp.float32)
    gate_part = gate_up[..., :hidden_width]
    up_part = gate_up[..., hidden_width:]
    sigmoid_g = jax.nn.sigmoid(gate_part)
    silu_g = gate_part * sigmoid_g
    activation = (silu_g * up_part).astype(jnp.bfloat16)
    d_gate = d_act * up_part * sigmoid_g * (1.0 + gate_part * (1.0 - sigmoid_g))
    d_up = d_act * silu_g
    payload = jnp.concatenate(
        [d_gate.astype(jnp.bfloat16), d_up.astype(jnp.bfloat16), activation], axis=-1
    )
    pay_shape = (home_slots, expert_peers, MOST, 3 * hidden_width)
    spread = jnp.transpose(payload.reshape(pay_shape), (1, 0, 2, 3))
    spread = lax.all_to_all(spread, "expert", split_axis=0, concat_axis=0, tiled=True)
    spread = spread.reshape(expert_peers * home_slots, MOST, 3 * hidden_width)
    spread = spread[inverse.reshape(expert_peers, home_slots)]
    spread = lax.all_to_all(spread, "expert", split_axis=0, concat_axis=0, tiled=True)
    mine_rows = jnp.transpose(spread, (1, 0, 2, 3)).reshape(
        home_slots, cell_count, 3 * hidden_width
    )

    d_gate_up = payload[..., : 2 * hidden_width]
    expert_out = jnp.einsum(
        "hrf,hfd->hrd", activation, full_dn, preferred_element_type=jnp.float32
    ).astype(jnp.bfloat16)
    d_rows = jnp.einsum(
        "hrf,hdf->hrd", d_gate_up, full_gu, preferred_element_type=jnp.float32
    ).astype(jnp.bfloat16)
    cells = (home_slots, expert_peers, MOST, model_width)
    scaled_out = cell_gate[..., None] * expert_out.reshape(cells).astype(jnp.float32)
    part_out = jnp.einsum(
        "shmt,hsmd->std",
        select.astype(jnp.float32),
        scaled_out,
        precision=lax.Precision.HIGHEST,
        preferred_element_type=jnp.float32,
    ).astype(jnp.bfloat16)
    part_grad = pick_rows("shmt,hsmd->std", select, d_rows.reshape(cells)).astype(jnp.bfloat16)
    sent = jnp.concatenate([part_out, part_grad], axis=-1)
    sent, mine_rows = lax.optimization_barrier((sent, mine_rows))
    back = lax.all_to_all(
        sent,
        "expert",
        split_axis=0,
        concat_axis=0,
        tiled=True,
    )
    summed = jnp.sum(back.astype(jnp.float32), axis=0).astype(jnp.bfloat16)
    layer_out = summed[:, :model_width]
    d_tokens = summed[:, model_width:]

    group_payload = lax.all_gather(mine_rows, "dp", axis=1, tiled=True)
    grad_gu = jnp.einsum(
        "hrc,hrf->hcf",
        new_tokens,
        group_payload[..., : 2 * hidden_width],
        preferred_element_type=jnp.float32,
    ).astype(jnp.bfloat16)
    grad_dn = jnp.einsum(
        "hrf,hrc->hfc",
        group_payload[..., 2 * hidden_width :],
        new_douts,
        preferred_element_type=jnp.float32,
    ).astype(jnp.bfloat16)
    return (layer_out, d_tokens, grad_gu, grad_dn)


def shards(tokens, expert_ids, *rest):
    if lax.axis_size("expert") < expert_ids.shape[1]:
        return shared_shards(tokens, expert_ids, *rest)
    return routed_shards(tokens, expert_ids, *rest)


def solution(mesh):
    return jax.shard_map(
        shards,
        mesh=mesh,
        in_specs=(
            P(("groups", "expert", "dp"), None),
            P(("groups", "expert", "dp"), None),
            P(("groups", "expert", "dp"), None),
            P("expert", "dp", None),
            P("expert", None, "dp"),
            P(),
            P(("groups", "expert", "dp"), None),
        ),
        out_specs=(
            P(("groups", "expert", "dp"), None),
            P(("groups", "expert", "dp"), None),
            P(("groups", "expert"), "dp", None),
            P(("groups", "expert"), None, "dp"),
        ),
        check_vma=False,
    )
```

```python
import jax
import jax.numpy as jnp
from jax import lax
from jax.sharding import PartitionSpec as P

MOST = 16
PARTS = 2


def relocate(gate_up, down, inverse):
    expert_peers = lax.axis_size("expert")
    home_slots = gate_up.shape[0]
    spread_gu = gate_up.reshape(
        home_slots, expert_peers, gate_up.shape[1] // expert_peers, gate_up.shape[2]
    )
    spread_dn = down.reshape(home_slots, expert_peers, down.shape[1] // expert_peers, down.shape[2])
    got_gu, got_dn = (
        lax.all_to_all(spread_gu, "expert", split_axis=1, concat_axis=0, tiled=True),
        lax.all_to_all(spread_dn, "expert", split_axis=1, concat_axis=0, tiled=True),
    )
    experts = home_slots * expert_peers
    slot_order = inverse.reshape(expert_peers, home_slots).T
    pick_gu = got_gu.reshape(experts, got_gu.shape[2], got_gu.shape[3])[slot_order]
    pick_dn = got_dn.reshape(experts, got_dn.shape[2], got_dn.shape[3])[slot_order]
    new_gu, new_dn = (
        lax.all_to_all(pick_gu, "expert", split_axis=1, concat_axis=1, tiled=True),
        lax.all_to_all(pick_dn, "expert", split_axis=1, concat_axis=1, tiled=True),
    )
    return (new_gu.reshape(gate_up.shape), new_dn.reshape(down.shape))


def route_cells(expert_ids, slot_map):
    experts = slot_map.shape[0]
    flat_ids = expert_ids.reshape(-1)
    matches = flat_ids[:, None] == jnp.arange(experts, dtype=jnp.int32)[None, :]
    indicator = matches.astype(jnp.int32)
    earlier = jnp.cumsum(indicator, axis=0) - indicator
    position = jnp.sum(jnp.where(matches, earlier, 0), axis=1)
    target = jnp.sum(jnp.where(matches, slot_map[None, :], 0), axis=1)
    target_cell = target * MOST + position
    entries = flat_ids.shape[0]
    source = (
        jnp.full((experts * MOST,), entries, jnp.int32)
        .at[target_cell]
        .set(jnp.arange(entries, dtype=jnp.int32))
    )
    return (target_cell, source)


def routed_shards(tokens, expert_ids, gate_values, w_gate_up, w_down, new_slot, cotangent):
    expert_peers = lax.axis_size("expert")
    home_slots = w_gate_up.shape[0]
    model_width = tokens.shape[1]
    hidden_width = w_down.shape[1]
    top_count = expert_ids.shape[1]
    token_count = tokens.shape[0]
    inverse = jnp.argsort(new_slot)
    local_gu, local_dn = relocate(w_gate_up, w_down, inverse)
    full_gu, full_dn = (
        lax.all_gather(local_gu, "dp", axis=1, tiled=True),
        lax.all_gather(local_dn, "dp", axis=2, tiled=True),
    )
    target_cell, source = route_cells(expert_ids, new_slot)
    blank_row = jnp.zeros((1, model_width), jnp.bfloat16)
    token_row = source // top_count
    cell_gates = jnp.concatenate([gate_values.reshape(-1), jnp.zeros((1,), jnp.float32)])[source]
    outgoing = jnp.concatenate([tokens, blank_row], axis=0)[token_row]
    cot_rows = jnp.concatenate([cotangent, blank_row], axis=0)[token_row]
    scaled_cot = (cell_gates[:, None] * cot_rows.astype(jnp.float32)).astype(jnp.bfloat16)
    row_shape = (expert_peers, home_slots, MOST, model_width)
    arrived = lax.all_to_all(
        outgoing.reshape(row_shape), "expert", split_axis=0, concat_axis=0, tiled=True
    )
    gate_up = jnp.einsum("shmd,hdf->shmf", arrived, full_gu, preferred_element_type=jnp.float32)
    gate_part = gate_up[..., :hidden_width]
    up_part = gate_up[..., hidden_width:]
    sigmoid_g = jax.nn.sigmoid(gate_part)
    silu_g = gate_part * sigmoid_g
    activation = (silu_g * up_part).astype(jnp.bfloat16)
    expert_out = jnp.einsum(
        "shmf,hfd->shmd", activation, full_dn, preferred_element_type=jnp.float32
    ).astype(jnp.bfloat16)
    returned = lax.all_to_all(expert_out, "expert", split_axis=0, concat_axis=0, tiled=True)
    gathered_out = returned.reshape(-1, model_width)[target_cell].reshape(
        token_count, top_count, model_width
    )
    layer_out = jnp.sum(gate_values[:, :, None] * gathered_out.astype(jnp.float32), axis=1).astype(
        jnp.bfloat16
    )
    d_outputs = lax.all_to_all(
        scaled_cot.reshape(row_shape), "expert", split_axis=0, concat_axis=0, tiled=True
    )
    d_act = jnp.einsum("shmd,hfd->shmf", d_outputs, full_dn, preferred_element_type=jnp.float32)
    d_gate = d_act * up_part * sigmoid_g * (1.0 + gate_part * (1.0 - sigmoid_g))
    d_up = d_act * silu_g
    d_gate_up = jnp.concatenate([d_gate, d_up], axis=-1).astype(jnp.bfloat16)
    d_rows = jnp.einsum(
        "shmf,hdf->shmd", d_gate_up, full_gu, preferred_element_type=jnp.float32
    ).astype(jnp.bfloat16)
    rows_back = lax.all_to_all(d_rows, "expert", split_axis=0, concat_axis=0, tiled=True)
    gathered_grads = rows_back.reshape(-1, model_width)[target_cell].reshape(
        token_count, top_count, model_width
    )
    d_tokens = jnp.sum(gathered_grads.astype(jnp.float32), axis=1).astype(jnp.bfloat16)
    part_gu = jnp.einsum("shmd,shmf->hdf", arrived, d_gate_up, preferred_element_type=jnp.float32)
    part_dn = jnp.einsum(
        "shmd,shmf->hdf", d_outputs, activation, preferred_element_type=jnp.float32
    )
    sum_gu, sum_dn = (
        lax.psum_scatter(
            part_gu.astype(jnp.bfloat16), "dp", scatter_dimension=1, tiled=True
        ).astype(jnp.float32),
        lax.psum_scatter(
            part_dn.astype(jnp.bfloat16), "dp", scatter_dimension=1, tiled=True
        ).astype(jnp.float32),
    )
    grad_gu = sum_gu.astype(jnp.bfloat16)
    grad_dn = jnp.swapaxes(sum_dn, 1, 2).astype(jnp.bfloat16)
    return (layer_out, d_tokens, grad_gu, grad_dn)


def cell_select(ids, gates, experts_here):
    match = ids[..., None] == experts_here
    member = jnp.any(match, axis=-2)
    gate = jnp.sum(jnp.where(match, gates[..., None], 0.0), axis=-2)
    count = ids.shape[-2]
    below = (jnp.arange(count)[:, None] > jnp.arange(count)[None, :]).astype(jnp.bfloat16)
    rank = jnp.einsum(
        "tu,...uh->...th",
        below,
        member.astype(jnp.bfloat16),
        preferred_element_type=jnp.float32,
    ).astype(jnp.int32)
    rank = jnp.where(member, rank, -1)
    rank = jnp.swapaxes(rank, -1, -2)
    gate = jnp.swapaxes(gate, -1, -2)
    select = rank[..., None, :] == jnp.arange(MOST, dtype=jnp.int32)[:, None]
    cell_gate = jnp.sum(jnp.where(select, gate[..., None, :], 0.0), axis=-1)
    return select, cell_gate


def pick_rows(spec, select, rows):
    return jnp.einsum(
        spec, select.astype(jnp.bfloat16), rows, preferred_element_type=jnp.float32
    )


def swap_pieces(rows, count, index):
    shape = rows.shape
    rows = rows.reshape(*shape[:-1], count // 2, 2, shape[-1] // count)
    rows = jnp.where(index % 2 == 1, rows[..., ::-1, :], rows)
    rows = jnp.where(index // 2 == 1, rows[..., ::-1, :, :], rows)
    return rows.reshape(shape)


def spread_weights(weight, part, half):
    group = lax.axis_index("groups")
    across = [(i, i ^ 1) for i in range(lax.axis_size("dp"))]
    beside = [(i, i ^ 2) for i in range(lax.axis_size("dp"))]
    weight = weight[2 * half * part : 2 * half * (part + 1)]
    pair = weight.reshape(2, half, *weight.shape[1:])
    own = jnp.where(group == 1, pair[::-1], pair)
    first = lax.ppermute(own[0], "dp", beside)
    own = own.reshape(weight.shape)
    core = lax.ppermute(own, "dp", across)
    second = lax.ppermute(first, "groups", [(0, 1), (1, 0)])
    chip = jnp.concatenate([first, second], axis=0)
    far = lax.ppermute(chip, "dp", across)
    return own, core, chip, far


def piece_columns(rows, index, share):
    return rows[..., index * share : (index + 1) * share]


def shared_shards(tokens, expert_ids, gate_values, w_gate_up, w_down, new_slot, cotangent):
    expert_peers = lax.axis_size("expert")
    dp_peers = lax.axis_size("dp")
    me = lax.axis_index("expert")
    home_slots = w_gate_up.shape[0]
    model_width = tokens.shape[1]
    hidden_width = w_down.shape[1]
    token_count = tokens.shape[0]
    share = model_width // dp_peers
    dp_index = lax.axis_index("dp")
    half = home_slots // (2 * PARTS)
    shift = lax.axis_index("groups") * half
    here = (me * home_slots + jnp.arange(home_slots, dtype=jnp.int32)) ^ shift

    both = jnp.concatenate(
        [swap_pieces(tokens, dp_peers, dp_index), swap_pieces(cotangent, dp_peers, dp_index)],
        axis=1,
    )
    rows_all = lax.all_gather(both, "expert", axis=0, tiled=False)
    ids_all = lax.all_gather(expert_ids, "expert", axis=0, tiled=False)
    gates_all = lax.all_gather(gate_values, "expert", axis=0, tiled=False)
    pieces = [
        (spread_weights(w_gate_up, part, half), spread_weights(w_down, part, half))
        for part in range(PARTS)
    ]

    select, cell_gate = cell_select(ids_all, gates_all, here)
    cell_rows = pick_rows("shmt,std->hsmd", select, rows_all)
    cell_gate = jnp.swapaxes(cell_gate, 0, 1)
    cell_count = expert_peers * MOST
    arrived = cell_rows[..., :model_width].astype(jnp.bfloat16)
    arrived = arrived.reshape(home_slots, cell_count, model_width)
    d_outputs = (cell_gate[..., None] * cell_rows[..., model_width:]).astype(jnp.bfloat16)
    d_outputs = d_outputs.reshape(home_slots, cell_count, model_width)

    inverse = jnp.argsort(new_slot).astype(jnp.int32)
    wide = rows_all.reshape(expert_peers, token_count, 2, model_width)
    wide = swap_pieces(wide, dp_peers, dp_index)
    wide = wide.reshape(expert_peers, token_count, 2, dp_peers, share)
    wide = jnp.transpose(wide, (3, 0, 1, 2, 4))
    narrow = lax.all_to_all(wide, "dp", split_axis=0, concat_axis=0, tiled=True)
    narrow = narrow.reshape(dp_peers, expert_peers, token_count, 2 * share)
    ids_group = lax.all_gather(ids_all, "dp", axis=0, tiled=False)
    gates_group = lax.all_gather(gates_all, "dp", axis=0, tiled=False)
    mine = lax.dynamic_slice_in_dim(inverse, me * home_slots, home_slots)
    select_new, gate_new = cell_select(ids_group, gates_group, mine)
    new_rows = pick_rows("pshmt,pstc->hpsmc", select_new, narrow)
    gate_new = jnp.transpose(gate_new, (2, 0, 1, 3))
    group_rows = dp_peers * cell_count
    new_tokens = new_rows[..., :share].astype(jnp.bfloat16)
    new_tokens = new_tokens.reshape(home_slots, group_rows, share)
    new_douts = (gate_new[..., None] * new_rows[..., share:]).astype(jnp.bfloat16)
    new_douts = new_douts.reshape(home_slots, group_rows, share)
    arrived, d_outputs, new_tokens, new_douts = lax.optimization_barrier(
        (arrived, d_outputs, new_tokens, new_douts)
    )

    payloads = []
    for part, (gu_pieces, dn_pieces) in enumerate(pieces):
        span = slice(2 * half * part, 2 * half * (part + 1))
        gate_up = sum(
            jnp.einsum(
                "hrd,hdf->hrf",
                piece_columns(arrived[span], index, share),
                gu_pieces[index],
                preferred_element_type=jnp.float32,
            )
            for index in range(dp_peers)
        )
        d_act = sum(
            jnp.einsum(
                "hrd,hfd->hrf",
                piece_columns(d_outputs[span], index, share),
                dn_pieces[index],
                preferred_element_type=jnp.float32,
            )
            for index in range(dp_peers)
        )
        gate_part = gate_up[..., :hidden_width]
        up_part = gate_up[..., hidden_width:]
        sigmoid_g = jax.nn.sigmoid(gate_part)
        silu_g = gate_part * sigmoid_g
        activation = (silu_g * up_part).astype(jnp.bfloat16)
        d_gate = d_act * up_part * sigmoid_g * (1.0 + gate_part * (1.0 - sigmoid_g))
        d_up = d_act * silu_g
        payloads.append(
            jnp.concatenate(
                [d_gate.astype(jnp.bfloat16), d_up.astype(jnp.bfloat16), activation], axis=-1
            )
        )
    payload = jnp.concatenate(payloads, axis=0)
    pay_shape = (home_slots, expert_peers, MOST, 3 * hidden_width)
    spread = jnp.transpose(payload.reshape(pay_shape), (1, 0, 2, 3))
    spread = lax.all_to_all(spread, "expert", split_axis=0, concat_axis=0, tiled=True)
    spread = spread.reshape(expert_peers * home_slots, MOST, 3 * hidden_width)
    spread = spread[(inverse ^ shift).reshape(expert_peers, home_slots)]
    spread = lax.all_to_all(spread, "expert", split_axis=0, concat_axis=0, tiled=True)
    mine_rows = jnp.transpose(spread, (1, 0, 2, 3)).reshape(
        home_slots, cell_count, 3 * hidden_width
    )

    outs, row_grads = [], []
    for part_payload, (gu_pieces, dn_pieces) in zip(payloads, pieces):
        outs.append(
            jnp.concatenate(
                [
                    jnp.einsum(
                        "hrf,hfd->hrd",
                        part_payload[..., 2 * hidden_width :],
                        piece,
                        preferred_element_type=jnp.float32,
                    ).astype(jnp.bfloat16)
                    for piece in dn_pieces
                ],
                axis=-1,
            )
        )
        row_grads.append(
            jnp.concatenate(
                [
                    jnp.einsum(
                        "hrf,hdf->hrd",
                        part_payload[..., : 2 * hidden_width],
                        piece,
                        preferred_element_type=jnp.float32,
                    ).astype(jnp.bfloat16)
                    for piece in gu_pieces
                ],
                axis=-1,
            )
        )
    expert_out = jnp.concatenate(outs, axis=0)
    d_rows = jnp.concatenate(row_grads, axis=0)
    cells = (home_slots, expert_peers, MOST, model_width)
    scaled_out = cell_gate[..., None] * expert_out.reshape(cells).astype(jnp.float32)
    part_out = jnp.einsum(
        "shmt,hsmd->std",
        select.astype(jnp.float32),
        scaled_out,
        precision=lax.Precision.HIGHEST,
        preferred_element_type=jnp.float32,
    ).astype(jnp.bfloat16)
    part_grad = pick_rows("shmt,hsmd->std", select, d_rows.reshape(cells)).astype(jnp.bfloat16)
    sent = jnp.concatenate([part_out, part_grad], axis=-1)
    sent, mine_rows = lax.optimization_barrier((sent, mine_rows))
    back = lax.all_to_all(
        sent,
        "expert",
        split_axis=0,
        concat_axis=0,
        tiled=True,
    )
    summed = jnp.sum(back.astype(jnp.float32), axis=0).astype(jnp.bfloat16)
    layer_out = swap_pieces(summed[:, :model_width], dp_peers, dp_index)
    d_tokens = swap_pieces(summed[:, model_width:], dp_peers, dp_index)

    group_payload = lax.all_gather(mine_rows, "dp", axis=1, tiled=True)
    grad_gu = jnp.einsum(
        "hrc,hrf->hcf",
        new_tokens,
        group_payload[..., : 2 * hidden_width],
        preferred_element_type=jnp.float32,
    ).astype(jnp.bfloat16)
    grad_dn = jnp.einsum(
        "hrf,hrc->hfc",
        group_payload[..., 2 * hidden_width :],
        new_douts,
        preferred_element_type=jnp.float32,
    ).astype(jnp.bfloat16)
    return (layer_out, d_tokens, grad_gu, grad_dn)


def shards(tokens, expert_ids, gate_values, w_gate_up, *rest):
    few_owners = lax.axis_size("expert") < expert_ids.shape[1]
    pairs = lax.axis_size("groups") == 2 and lax.axis_size("dp") == 4
    half = w_gate_up.shape[0] // (2 * PARTS)
    even = w_gate_up.shape[0] == 2 * PARTS * half and half > 0 and half & (half - 1) == 0
    body = shared_shards if few_owners and pairs and even else routed_shards
    return body(tokens, expert_ids, gate_values, w_gate_up, *rest)


def solution(mesh):
    return jax.shard_map(
        shards,
        mesh=mesh,
        in_specs=(
            P(("groups", "expert", "dp"), None),
            P(("groups", "expert", "dp"), None),
            P(("groups", "expert", "dp"), None),
            P("expert", "dp", None),
            P("expert", None, "dp"),
            P(),
            P(("groups", "expert", "dp"), None),
        ),
        out_specs=(
            P(("groups", "expert", "dp"), None),
            P(("groups", "expert", "dp"), None),
            P(("groups", "expert"), "dp", None),
            P(("groups", "expert"), None, "dp"),
        ),
        check_vma=False,
    )
```

```python
import jax
import jax.numpy as jnp
from jax import lax
from jax.sharding import PartitionSpec as P

MOST = 16
PARTS = 2


def relocate(gate_up, down, inverse):
    expert_peers = lax.axis_size("expert")
    home_slots = gate_up.shape[0]
    spread_gu = gate_up.reshape(
        home_slots, expert_peers, gate_up.shape[1] // expert_peers, gate_up.shape[2]
    )
    spread_dn = down.reshape(home_slots, expert_peers, down.shape[1] // expert_peers, down.shape[2])
    got_gu, got_dn = (
        lax.all_to_all(spread_gu, "expert", split_axis=1, concat_axis=0, tiled=True),
        lax.all_to_all(spread_dn, "expert", split_axis=1, concat_axis=0, tiled=True),
    )
    experts = home_slots * expert_peers
    slot_order = inverse.reshape(expert_peers, home_slots).T
    pick_gu = got_gu.reshape(experts, got_gu.shape[2], got_gu.shape[3])[slot_order]
    pick_dn = got_dn.reshape(experts, got_dn.shape[2], got_dn.shape[3])[slot_order]
    new_gu, new_dn = (
        lax.all_to_all(pick_gu, "expert", split_axis=1, concat_axis=1, tiled=True),
        lax.all_to_all(pick_dn, "expert", split_axis=1, concat_axis=1, tiled=True),
    )
    return (new_gu.reshape(gate_up.shape), new_dn.reshape(down.shape))


def route_cells(expert_ids, slot_map):
    experts = slot_map.shape[0]
    flat_ids = expert_ids.reshape(-1)
    matches = flat_ids[:, None] == jnp.arange(experts, dtype=jnp.int32)[None, :]
    indicator = matches.astype(jnp.int32)
    earlier = jnp.cumsum(indicator, axis=0) - indicator
    position = jnp.sum(jnp.where(matches, earlier, 0), axis=1)
    target = jnp.sum(jnp.where(matches, slot_map[None, :], 0), axis=1)
    target_cell = target * MOST + position
    entries = flat_ids.shape[0]
    source = (
        jnp.full((experts * MOST,), entries, jnp.int32)
        .at[target_cell]
        .set(jnp.arange(entries, dtype=jnp.int32))
    )
    return (target_cell, source)


def routed_shards(tokens, expert_ids, gate_values, w_gate_up, w_down, new_slot, cotangent):
    expert_peers = lax.axis_size("expert")
    home_slots = w_gate_up.shape[0]
    model_width = tokens.shape[1]
    hidden_width = w_down.shape[1]
    top_count = expert_ids.shape[1]
    token_count = tokens.shape[0]
    inverse = jnp.argsort(new_slot)
    local_gu, local_dn = relocate(w_gate_up, w_down, inverse)
    full_gu, full_dn = (
        lax.all_gather(local_gu, "dp", axis=1, tiled=True),
        lax.all_gather(local_dn, "dp", axis=2, tiled=True),
    )
    target_cell, source = route_cells(expert_ids, new_slot)
    blank_row = jnp.zeros((1, model_width), jnp.bfloat16)
    token_row = source // top_count
    cell_gates = jnp.concatenate([gate_values.reshape(-1), jnp.zeros((1,), jnp.float32)])[source]
    outgoing = jnp.concatenate([tokens, blank_row], axis=0)[token_row]
    cot_rows = jnp.concatenate([cotangent, blank_row], axis=0)[token_row]
    scaled_cot = (cell_gates[:, None] * cot_rows.astype(jnp.float32)).astype(jnp.bfloat16)
    row_shape = (expert_peers, home_slots, MOST, model_width)
    arrived = lax.all_to_all(
        outgoing.reshape(row_shape), "expert", split_axis=0, concat_axis=0, tiled=True
    )
    gate_up = jnp.einsum("shmd,hdf->shmf", arrived, full_gu, preferred_element_type=jnp.float32)
    gate_part = gate_up[..., :hidden_width]
    up_part = gate_up[..., hidden_width:]
    sigmoid_g = jax.nn.sigmoid(gate_part)
    silu_g = gate_part * sigmoid_g
    activation = (silu_g * up_part).astype(jnp.bfloat16)
    expert_out = jnp.einsum(
        "shmf,hfd->shmd", activation, full_dn, preferred_element_type=jnp.float32
    ).astype(jnp.bfloat16)
    returned = lax.all_to_all(expert_out, "expert", split_axis=0, concat_axis=0, tiled=True)
    gathered_out = returned.reshape(-1, model_width)[target_cell].reshape(
        token_count, top_count, model_width
    )
    layer_out = jnp.sum(gate_values[:, :, None] * gathered_out.astype(jnp.float32), axis=1).astype(
        jnp.bfloat16
    )
    d_outputs = lax.all_to_all(
        scaled_cot.reshape(row_shape), "expert", split_axis=0, concat_axis=0, tiled=True
    )
    d_act = jnp.einsum("shmd,hfd->shmf", d_outputs, full_dn, preferred_element_type=jnp.float32)
    d_gate = d_act * up_part * sigmoid_g * (1.0 + gate_part * (1.0 - sigmoid_g))
    d_up = d_act * silu_g
    d_gate_up = jnp.concatenate([d_gate, d_up], axis=-1).astype(jnp.bfloat16)
    d_rows = jnp.einsum(
        "shmf,hdf->shmd", d_gate_up, full_gu, preferred_element_type=jnp.float32
    ).astype(jnp.bfloat16)
    rows_back = lax.all_to_all(d_rows, "expert", split_axis=0, concat_axis=0, tiled=True)
    gathered_grads = rows_back.reshape(-1, model_width)[target_cell].reshape(
        token_count, top_count, model_width
    )
    d_tokens = jnp.sum(gathered_grads.astype(jnp.float32), axis=1).astype(jnp.bfloat16)
    part_gu = jnp.einsum("shmd,shmf->hdf", arrived, d_gate_up, preferred_element_type=jnp.float32)
    part_dn = jnp.einsum(
        "shmd,shmf->hdf", d_outputs, activation, preferred_element_type=jnp.float32
    )
    sum_gu, sum_dn = (
        lax.psum_scatter(
            part_gu.astype(jnp.bfloat16), "dp", scatter_dimension=1, tiled=True
        ).astype(jnp.float32),
        lax.psum_scatter(
            part_dn.astype(jnp.bfloat16), "dp", scatter_dimension=1, tiled=True
        ).astype(jnp.float32),
    )
    grad_gu = sum_gu.astype(jnp.bfloat16)
    grad_dn = jnp.swapaxes(sum_dn, 1, 2).astype(jnp.bfloat16)
    return (layer_out, d_tokens, grad_gu, grad_dn)


def cell_select(ids, gates, experts_here):
    match = ids[..., None] == experts_here
    member = jnp.any(match, axis=-2)
    gate = jnp.sum(jnp.where(match, gates[..., None], 0.0), axis=-2)
    count = ids.shape[-2]
    below = (jnp.arange(count)[:, None] > jnp.arange(count)[None, :]).astype(jnp.bfloat16)
    rank = jnp.einsum(
        "tu,...uh->...th",
        below,
        member.astype(jnp.bfloat16),
        preferred_element_type=jnp.float32,
    ).astype(jnp.int32)
    rank = jnp.where(member, rank, -1)
    rank = jnp.swapaxes(rank, -1, -2)
    gate = jnp.swapaxes(gate, -1, -2)
    select = rank[..., None, :] == jnp.arange(MOST, dtype=jnp.int32)[:, None]
    cell_gate = jnp.sum(jnp.where(select, gate[..., None, :], 0.0), axis=-1)
    return select, cell_gate


def pick_rows(spec, select, rows):
    return jnp.einsum(
        spec, select.astype(jnp.bfloat16), rows, preferred_element_type=jnp.float32
    )


def swap_pieces(rows, count, index):
    shape = rows.shape
    rows = rows.reshape(*shape[:-1], count // 2, 2, shape[-1] // count)
    rows = jnp.where(index % 2 == 1, rows[..., ::-1, :], rows)
    rows = jnp.where(index // 2 == 1, rows[..., ::-1, :, :], rows)
    return rows.reshape(shape)


def spread_weights(weight, part, half):
    group = lax.axis_index("groups")
    across = [(i, i ^ 1) for i in range(lax.axis_size("dp"))]
    beside = [(i, i ^ 2) for i in range(lax.axis_size("dp"))]
    weight = weight[2 * half * part : 2 * half * (part + 1)]
    pair = weight.reshape(2, half, *weight.shape[1:])
    own = jnp.where(group == 1, pair[::-1], pair)
    first = lax.ppermute(own[0], "dp", beside)
    own = own.reshape(weight.shape)
    core = lax.ppermute(own, "dp", across)
    second = lax.ppermute(first, "groups", [(0, 1), (1, 0)])
    chip = jnp.concatenate([first, second], axis=0)
    far = lax.ppermute(chip, "dp", across)
    return own, core, chip, far


def piece_columns(rows, index, share):
    return rows[..., index * share : (index + 1) * share]


def shared_shards(tokens, expert_ids, gate_values, w_gate_up, w_down, new_slot, cotangent):
    expert_peers = lax.axis_size("expert")
    dp_peers = lax.axis_size("dp")
    me = lax.axis_index("expert")
    home_slots = w_gate_up.shape[0]
    model_width = tokens.shape[1]
    hidden_width = w_down.shape[1]
    token_count = tokens.shape[0]
    share = model_width // dp_peers
    dp_index = lax.axis_index("dp")
    half = home_slots // (2 * PARTS)
    shift = lax.axis_index("groups") * half
    here = (me * home_slots + jnp.arange(home_slots, dtype=jnp.int32)) ^ shift

    both = jnp.concatenate(
        [swap_pieces(tokens, dp_peers, dp_index), swap_pieces(cotangent, dp_peers, dp_index)],
        axis=1,
    )
    rows_all = lax.all_gather(both, "expert", axis=0, tiled=False)
    routing = jnp.concatenate([expert_ids.astype(jnp.float32).T, gate_values.T], axis=0)
    routing = lax.all_gather(routing, ("expert", "dp"), axis=0, tiled=False)
    routing, w_gate_up, w_down = lax.optimization_barrier((routing, w_gate_up, w_down))
    routing = routing.reshape(expert_peers, dp_peers, *routing.shape[1:])
    routing = jnp.transpose(routing, (1, 0, 3, 2))
    top_count = expert_ids.shape[1]
    ids_group = routing[..., :top_count].astype(jnp.int32)
    gates_group = routing[..., top_count:]
    ids_all = lax.dynamic_index_in_dim(ids_group, dp_index, 0, keepdims=False)
    gates_all = lax.dynamic_index_in_dim(gates_group, dp_index, 0, keepdims=False)
    pieces = [
        (spread_weights(w_gate_up, part, half), spread_weights(w_down, part, half))
        for part in range(PARTS)
    ]

    select, cell_gate = cell_select(ids_all, gates_all, here)
    cell_rows = pick_rows("shmt,std->hsmd", select, rows_all)
    cell_gate = jnp.swapaxes(cell_gate, 0, 1)
    cell_count = expert_peers * MOST
    arrived = cell_rows[..., :model_width].astype(jnp.bfloat16)
    arrived = arrived.reshape(home_slots, cell_count, model_width)
    d_outputs = (cell_gate[..., None] * cell_rows[..., model_width:]).astype(jnp.bfloat16)
    d_outputs = d_outputs.reshape(home_slots, cell_count, model_width)

    inverse = jnp.argsort(new_slot).astype(jnp.int32)
    mine = lax.dynamic_slice_in_dim(inverse, me * home_slots, home_slots)
    payloads = []
    for part, (gu_pieces, dn_pieces) in enumerate(pieces):
        span = slice(2 * half * part, 2 * half * (part + 1))
        gate_up = sum(
            jnp.einsum(
                "hrd,hdf->hrf",
                piece_columns(arrived[span], index, share),
                gu_pieces[index],
                preferred_element_type=jnp.float32,
            )
            for index in range(dp_peers)
        )
        d_act = sum(
            jnp.einsum(
                "hrd,hfd->hrf",
                piece_columns(d_outputs[span], index, share),
                dn_pieces[index],
                preferred_element_type=jnp.float32,
            )
            for index in range(dp_peers)
        )
        gate_part = gate_up[..., :hidden_width]
        up_part = gate_up[..., hidden_width:]
        sigmoid_g = jax.nn.sigmoid(gate_part)
        silu_g = gate_part * sigmoid_g
        activation = (silu_g * up_part).astype(jnp.bfloat16)
        d_gate = d_act * up_part * sigmoid_g * (1.0 + gate_part * (1.0 - sigmoid_g))
        d_up = d_act * silu_g
        payloads.append(
            jnp.concatenate(
                [d_gate.astype(jnp.bfloat16), d_up.astype(jnp.bfloat16), activation], axis=-1
            )
        )
    last = payloads[-1]
    rows_all, last = lax.optimization_barrier((rows_all, last))
    payloads[-1] = last
    wide = rows_all.reshape(expert_peers, token_count, 2, dp_peers, share)
    narrow = [wide[..., 0, :]]
    for index in range(1, dp_peers):
        partners = [(i, i ^ index) for i in range(dp_peers)]
        narrow.append(lax.ppermute(wide[..., index, :], "dp", partners))
    narrow = jnp.stack(narrow).reshape(dp_peers // 2, 2, expert_peers, token_count, 2 * share)
    narrow = jnp.where(dp_index % 2 == 1, narrow[:, ::-1], narrow)
    narrow = jnp.where(dp_index // 2 == 1, narrow[::-1], narrow)
    narrow = narrow.reshape(dp_peers, expert_peers, token_count, 2 * share)
    select_new, gate_new = cell_select(ids_group, gates_group, mine)
    new_rows = pick_rows("pshmt,pstc->hpsmc", select_new, narrow)
    gate_new = jnp.transpose(gate_new, (2, 0, 1, 3))
    group_rows = dp_peers * cell_count
    new_tokens = new_rows[..., :share].astype(jnp.bfloat16)
    new_tokens = new_tokens.reshape(home_slots, group_rows, share)
    new_douts = (gate_new[..., None] * new_rows[..., share:]).astype(jnp.bfloat16)
    new_douts = new_douts.reshape(home_slots, group_rows, share)
    pay_shape = (2 * half, expert_peers, MOST, 3 * hidden_width)
    spread = jnp.concatenate(
        [
            lax.all_to_all(
                jnp.transpose(part_payload.reshape(pay_shape), (1, 0, 2, 3)),
                "expert",
                split_axis=0,
                concat_axis=0,
                tiled=True,
            )
            for part_payload in payloads
        ],
        axis=1,
    )
    spread = spread.reshape(expert_peers * home_slots, MOST, 3 * hidden_width)
    spread = spread[(inverse ^ shift).reshape(expert_peers, home_slots)]
    spread = lax.all_to_all(spread, "expert", split_axis=0, concat_axis=0, tiled=True)
    mine_rows = jnp.transpose(spread, (1, 0, 2, 3)).reshape(
        home_slots, cell_count, 3 * hidden_width
    )

    outs, row_grads = [], []
    for part_payload, (gu_pieces, dn_pieces) in zip(payloads, pieces):
        outs.append(
            jnp.concatenate(
                [
                    jnp.einsum(
                        "hrf,hfd->hrd",
                        part_payload[..., 2 * hidden_width :],
                        piece,
                        preferred_element_type=jnp.float32,
                    ).astype(jnp.bfloat16)
                    for piece in dn_pieces
                ],
                axis=-1,
            )
        )
        row_grads.append(
            jnp.concatenate(
                [
                    jnp.einsum(
                        "hrf,hdf->hrd",
                        part_payload[..., : 2 * hidden_width],
                        piece,
                        preferred_element_type=jnp.float32,
                    ).astype(jnp.bfloat16)
                    for piece in gu_pieces
                ],
                axis=-1,
            )
        )
    expert_out = jnp.concatenate(outs, axis=0)
    d_rows = jnp.concatenate(row_grads, axis=0)
    cells = (home_slots, expert_peers, MOST, model_width)
    scaled_out = cell_gate[..., None] * expert_out.reshape(cells).astype(jnp.float32)
    part_out = jnp.einsum(
        "shmt,hsmd->std",
        select.astype(jnp.float32),
        scaled_out,
        precision=lax.Precision.HIGHEST,
        preferred_element_type=jnp.float32,
    ).astype(jnp.bfloat16)
    part_grad = pick_rows("shmt,hsmd->std", select, d_rows.reshape(cells)).astype(jnp.bfloat16)
    sent = jnp.concatenate([part_out, part_grad], axis=-1)
    sent, mine_rows = lax.optimization_barrier((sent, mine_rows))
    back = lax.all_to_all(
        sent,
        "expert",
        split_axis=0,
        concat_axis=0,
        tiled=True,
    )
    summed = jnp.sum(back.astype(jnp.float32), axis=0).astype(jnp.bfloat16)
    layer_out = swap_pieces(summed[:, :model_width], dp_peers, dp_index)
    d_tokens = swap_pieces(summed[:, model_width:], dp_peers, dp_index)

    group_payload = lax.all_gather(mine_rows, "dp", axis=1, tiled=True)
    grad_gu = jnp.einsum(
        "hrc,hrf->hcf",
        new_tokens,
        group_payload[..., : 2 * hidden_width],
        preferred_element_type=jnp.float32,
    ).astype(jnp.bfloat16)
    grad_dn = jnp.einsum(
        "hrf,hrc->hfc",
        group_payload[..., 2 * hidden_width :],
        new_douts,
        preferred_element_type=jnp.float32,
    ).astype(jnp.bfloat16)
    return (layer_out, d_tokens, grad_gu, grad_dn)


def shards(tokens, expert_ids, gate_values, w_gate_up, *rest):
    few_owners = lax.axis_size("expert") < expert_ids.shape[1]
    pairs = lax.axis_size("groups") == 2 and lax.axis_size("dp") == 4
    half = w_gate_up.shape[0] // (2 * PARTS)
    even = w_gate_up.shape[0] == 2 * PARTS * half and half > 0 and half & (half - 1) == 0
    body = shared_shards if few_owners and pairs and even else routed_shards
    return body(tokens, expert_ids, gate_values, w_gate_up, *rest)


def solution(mesh):
    return jax.shard_map(
        shards,
        mesh=mesh,
        in_specs=(
            P(("groups", "expert", "dp"), None),
            P(("groups", "expert", "dp"), None),
            P(("groups", "expert", "dp"), None),
            P("expert", "dp", None),
            P("expert", None, "dp"),
            P(),
            P(("groups", "expert", "dp"), None),
        ),
        out_specs=(
            P(("groups", "expert", "dp"), None),
            P(("groups", "expert", "dp"), None),
            P(("groups", "expert"), "dp", None),
            P(("groups", "expert"), None, "dp"),
        ),
        check_vma=False,
    )
```

```python
import jax
import jax.numpy as jnp
from jax import lax
from jax.sharding import PartitionSpec as P

MOST = 16
PARTS = 2


def relocate(gate_up, down, inverse):
    expert_peers = lax.axis_size("expert")
    home_slots = gate_up.shape[0]
    spread_gu = gate_up.reshape(
        home_slots, expert_peers, gate_up.shape[1] // expert_peers, gate_up.shape[2]
    )
    spread_dn = down.reshape(home_slots, expert_peers, down.shape[1] // expert_peers, down.shape[2])
    got_gu, got_dn = (
        lax.all_to_all(spread_gu, "expert", split_axis=1, concat_axis=0, tiled=True),
        lax.all_to_all(spread_dn, "expert", split_axis=1, concat_axis=0, tiled=True),
    )
    experts = home_slots * expert_peers
    slot_order = inverse.reshape(expert_peers, home_slots).T
    pick_gu = got_gu.reshape(experts, got_gu.shape[2], got_gu.shape[3])[slot_order]
    pick_dn = got_dn.reshape(experts, got_dn.shape[2], got_dn.shape[3])[slot_order]
    new_gu, new_dn = (
        lax.all_to_all(pick_gu, "expert", split_axis=1, concat_axis=1, tiled=True),
        lax.all_to_all(pick_dn, "expert", split_axis=1, concat_axis=1, tiled=True),
    )
    return (new_gu.reshape(gate_up.shape), new_dn.reshape(down.shape))


def route_cells(expert_ids, slot_map):
    experts = slot_map.shape[0]
    flat_ids = expert_ids.reshape(-1)
    matches = flat_ids[:, None] == jnp.arange(experts, dtype=jnp.int32)[None, :]
    indicator = matches.astype(jnp.int32)
    earlier = jnp.cumsum(indicator, axis=0) - indicator
    position = jnp.sum(jnp.where(matches, earlier, 0), axis=1)
    target = jnp.sum(jnp.where(matches, slot_map[None, :], 0), axis=1)
    target_cell = target * MOST + position
    entries = flat_ids.shape[0]
    source = (
        jnp.full((experts * MOST,), entries, jnp.int32)
        .at[target_cell]
        .set(jnp.arange(entries, dtype=jnp.int32))
    )
    return (target_cell, source)


def routed_shards(tokens, expert_ids, gate_values, w_gate_up, w_down, new_slot, cotangent):
    expert_peers = lax.axis_size("expert")
    home_slots = w_gate_up.shape[0]
    model_width = tokens.shape[1]
    hidden_width = w_down.shape[1]
    top_count = expert_ids.shape[1]
    token_count = tokens.shape[0]
    inverse = jnp.argsort(new_slot)
    local_gu, local_dn = relocate(w_gate_up, w_down, inverse)
    full_gu, full_dn = (
        lax.all_gather(local_gu, "dp", axis=1, tiled=True),
        lax.all_gather(local_dn, "dp", axis=2, tiled=True),
    )
    target_cell, source = route_cells(expert_ids, new_slot)
    blank_row = jnp.zeros((1, model_width), jnp.bfloat16)
    token_row = source // top_count
    cell_gates = jnp.concatenate([gate_values.reshape(-1), jnp.zeros((1,), jnp.float32)])[source]
    outgoing = jnp.concatenate([tokens, blank_row], axis=0)[token_row]
    cot_rows = jnp.concatenate([cotangent, blank_row], axis=0)[token_row]
    scaled_cot = (cell_gates[:, None] * cot_rows.astype(jnp.float32)).astype(jnp.bfloat16)
    row_shape = (expert_peers, home_slots, MOST, model_width)
    arrived = lax.all_to_all(
        outgoing.reshape(row_shape), "expert", split_axis=0, concat_axis=0, tiled=True
    )
    gate_up = jnp.einsum("shmd,hdf->shmf", arrived, full_gu, preferred_element_type=jnp.float32)
    gate_part = gate_up[..., :hidden_width]
    up_part = gate_up[..., hidden_width:]
    sigmoid_g = jax.nn.sigmoid(gate_part)
    silu_g = gate_part * sigmoid_g
    activation = (silu_g * up_part).astype(jnp.bfloat16)
    expert_out = jnp.einsum(
        "shmf,hfd->shmd", activation, full_dn, preferred_element_type=jnp.float32
    ).astype(jnp.bfloat16)
    returned = lax.all_to_all(expert_out, "expert", split_axis=0, concat_axis=0, tiled=True)
    gathered_out = returned.reshape(-1, model_width)[target_cell].reshape(
        token_count, top_count, model_width
    )
    layer_out = jnp.sum(gate_values[:, :, None] * gathered_out.astype(jnp.float32), axis=1).astype(
        jnp.bfloat16
    )
    d_outputs = lax.all_to_all(
        scaled_cot.reshape(row_shape), "expert", split_axis=0, concat_axis=0, tiled=True
    )
    d_act = jnp.einsum("shmd,hfd->shmf", d_outputs, full_dn, preferred_element_type=jnp.float32)
    d_gate = d_act * up_part * sigmoid_g * (1.0 + gate_part * (1.0 - sigmoid_g))
    d_up = d_act * silu_g
    d_gate_up = jnp.concatenate([d_gate, d_up], axis=-1).astype(jnp.bfloat16)
    d_rows = jnp.einsum(
        "shmf,hdf->shmd", d_gate_up, full_gu, preferred_element_type=jnp.float32
    ).astype(jnp.bfloat16)
    rows_back = lax.all_to_all(d_rows, "expert", split_axis=0, concat_axis=0, tiled=True)
    gathered_grads = rows_back.reshape(-1, model_width)[target_cell].reshape(
        token_count, top_count, model_width
    )
    d_tokens = jnp.sum(gathered_grads.astype(jnp.float32), axis=1).astype(jnp.bfloat16)
    part_gu = jnp.einsum("shmd,shmf->hdf", arrived, d_gate_up, preferred_element_type=jnp.float32)
    part_dn = jnp.einsum(
        "shmd,shmf->hdf", d_outputs, activation, preferred_element_type=jnp.float32
    )
    sum_gu, sum_dn = (
        lax.psum_scatter(
            part_gu.astype(jnp.bfloat16), "dp", scatter_dimension=1, tiled=True
        ).astype(jnp.float32),
        lax.psum_scatter(
            part_dn.astype(jnp.bfloat16), "dp", scatter_dimension=1, tiled=True
        ).astype(jnp.float32),
    )
    grad_gu = sum_gu.astype(jnp.bfloat16)
    grad_dn = jnp.swapaxes(sum_dn, 1, 2).astype(jnp.bfloat16)
    return (layer_out, d_tokens, grad_gu, grad_dn)


def cell_select(ids, gates, experts_here):
    match = ids[..., None] == experts_here
    member = jnp.any(match, axis=-2)
    gate = jnp.sum(jnp.where(match, gates[..., None], 0.0), axis=-2)
    count = ids.shape[-2]
    below = (jnp.arange(count)[:, None] > jnp.arange(count)[None, :]).astype(jnp.bfloat16)
    rank = jnp.einsum(
        "tu,...uh->...th",
        below,
        member.astype(jnp.bfloat16),
        preferred_element_type=jnp.float32,
    ).astype(jnp.int32)
    rank = jnp.where(member, rank, -1)
    rank = jnp.swapaxes(rank, -1, -2)
    gate = jnp.swapaxes(gate, -1, -2)
    select = rank[..., None, :] == jnp.arange(MOST, dtype=jnp.int32)[:, None]
    cell_gate = jnp.sum(jnp.where(select, gate[..., None, :], 0.0), axis=-1)
    return select, cell_gate


def pick_rows(spec, select, rows):
    return jnp.einsum(
        spec, select.astype(jnp.bfloat16), rows, preferred_element_type=jnp.float32
    )


def swap_pieces(rows, count, index):
    shape = rows.shape
    rows = rows.reshape(*shape[:-1], count // 2, 2, shape[-1] // count)
    rows = jnp.where(index % 2 == 1, rows[..., ::-1, :], rows)
    rows = jnp.where(index // 2 == 1, rows[..., ::-1, :, :], rows)
    return rows.reshape(shape)


def spread_weights(weight, part, half, previous):
    group = lax.axis_index("groups")
    across = [(i, i ^ 1) for i in range(lax.axis_size("dp"))]
    beside = [(i, i ^ 2) for i in range(lax.axis_size("dp"))]
    weight = weight[2 * half * part : 2 * half * (part + 1)]
    pair = weight.reshape(2, half, *weight.shape[1:])
    own = jnp.where(group == 1, pair[::-1], pair)
    near = own[0]
    if previous is not None:
        near, previous = lax.optimization_barrier((near, previous))
    first = lax.ppermute(near, "dp", beside)
    own = own.reshape(weight.shape)
    core = lax.ppermute(own, "dp", across)
    second = lax.ppermute(first, "groups", [(0, 1), (1, 0)])
    chip = jnp.concatenate([first, second], axis=0)
    far = lax.ppermute(chip, "dp", across)
    return (own, core, chip, far), first


def piece_columns(rows, index, share):
    return rows[..., index * share : (index + 1) * share]


def shared_shards(tokens, expert_ids, gate_values, w_gate_up, w_down, new_slot, cotangent):
    expert_peers = lax.axis_size("expert")
    dp_peers = lax.axis_size("dp")
    me = lax.axis_index("expert")
    home_slots = w_gate_up.shape[0]
    model_width = tokens.shape[1]
    hidden_width = w_down.shape[1]
    token_count = tokens.shape[0]
    share = model_width // dp_peers
    dp_index = lax.axis_index("dp")
    half = home_slots // (2 * PARTS)
    shift = lax.axis_index("groups") * half
    here = (me * home_slots + jnp.arange(home_slots, dtype=jnp.int32)) ^ shift

    both = jnp.concatenate(
        [swap_pieces(tokens, dp_peers, dp_index), swap_pieces(cotangent, dp_peers, dp_index)],
        axis=1,
    )
    rows_all = lax.all_gather(both, "expert", axis=0, tiled=False)
    routing = jnp.concatenate([expert_ids.astype(jnp.float32).T, gate_values.T], axis=0)
    routing = lax.all_gather(routing, ("expert", "dp"), axis=0, tiled=False)
    routing, w_gate_up, w_down = lax.optimization_barrier((routing, w_gate_up, w_down))
    routing = routing.reshape(expert_peers, dp_peers, *routing.shape[1:])
    routing = jnp.transpose(routing, (1, 0, 3, 2))
    top_count = expert_ids.shape[1]
    ids_group = routing[..., :top_count].astype(jnp.int32)
    gates_group = routing[..., top_count:]
    ids_all = lax.dynamic_index_in_dim(ids_group, dp_index, 0, keepdims=False)
    gates_all = lax.dynamic_index_in_dim(gates_group, dp_index, 0, keepdims=False)
    pieces = []
    previous = None
    for part in range(PARTS):
        gu_pieces, previous = spread_weights(w_gate_up, part, half, previous)
        dn_pieces, previous = spread_weights(w_down, part, half, previous)
        pieces.append((gu_pieces, dn_pieces))

    select, cell_gate = cell_select(ids_all, gates_all, here)
    cell_rows = pick_rows("shmt,std->hsmd", select, rows_all)
    cell_gate = jnp.swapaxes(cell_gate, 0, 1)
    cell_count = expert_peers * MOST
    arrived = cell_rows[..., :model_width].astype(jnp.bfloat16)
    arrived = arrived.reshape(home_slots, cell_count, model_width)
    d_outputs = (cell_gate[..., None] * cell_rows[..., model_width:]).astype(jnp.bfloat16)
    d_outputs = d_outputs.reshape(home_slots, cell_count, model_width)

    inverse = jnp.argsort(new_slot).astype(jnp.int32)
    mine = lax.dynamic_slice_in_dim(inverse, me * home_slots, home_slots)
    payloads = []
    for part, (gu_pieces, dn_pieces) in enumerate(pieces):
        span = slice(2 * half * part, 2 * half * (part + 1))
        gate_up = sum(
            jnp.einsum(
                "hrd,hdf->hrf",
                piece_columns(arrived[span], index, share),
                gu_pieces[index],
                preferred_element_type=jnp.float32,
            )
            for index in range(dp_peers)
        )
        d_act = sum(
            jnp.einsum(
                "hrd,hfd->hrf",
                piece_columns(d_outputs[span], index, share),
                dn_pieces[index],
                preferred_element_type=jnp.float32,
            )
            for index in range(dp_peers)
        )
        gate_part = gate_up[..., :hidden_width]
        up_part = gate_up[..., hidden_width:]
        sigmoid_g = jax.nn.sigmoid(gate_part)
        silu_g = gate_part * sigmoid_g
        activation = (silu_g * up_part).astype(jnp.bfloat16)
        d_gate = d_act * up_part * sigmoid_g * (1.0 + gate_part * (1.0 - sigmoid_g))
        d_up = d_act * silu_g
        payloads.append(
            jnp.concatenate(
                [d_gate.astype(jnp.bfloat16), d_up.astype(jnp.bfloat16), activation], axis=-1
            )
        )
    rows_all, previous = lax.optimization_barrier((rows_all, previous))
    wide = rows_all.reshape(expert_peers, token_count, 2, dp_peers, share)
    narrow = [wide[..., 0, :]]
    for index in range(1, dp_peers):
        partners = [(i, i ^ index) for i in range(dp_peers)]
        narrow.append(lax.ppermute(wide[..., index, :], "dp", partners))
    narrow = jnp.stack(narrow).reshape(dp_peers // 2, 2, expert_peers, token_count, 2 * share)
    narrow = jnp.where(dp_index % 2 == 1, narrow[:, ::-1], narrow)
    narrow = jnp.where(dp_index // 2 == 1, narrow[::-1], narrow)
    narrow = narrow.reshape(dp_peers, expert_peers, token_count, 2 * share)
    select_new, gate_new = cell_select(ids_group, gates_group, mine)
    new_rows = pick_rows("pshmt,pstc->hpsmc", select_new, narrow)
    gate_new = jnp.transpose(gate_new, (2, 0, 1, 3))
    group_rows = dp_peers * cell_count
    new_tokens = new_rows[..., :share].astype(jnp.bfloat16)
    new_tokens = new_tokens.reshape(home_slots, group_rows, share)
    new_douts = (gate_new[..., None] * new_rows[..., share:]).astype(jnp.bfloat16)
    new_douts = new_douts.reshape(home_slots, group_rows, share)
    pay_shape = (2 * half, expert_peers, MOST, 3 * hidden_width)
    spread = jnp.concatenate(
        [
            lax.all_to_all(
                jnp.transpose(part_payload.reshape(pay_shape), (1, 0, 2, 3)),
                "expert",
                split_axis=0,
                concat_axis=0,
                tiled=True,
            )
            for part_payload in payloads
        ],
        axis=1,
    )
    spread = spread.reshape(expert_peers * home_slots, MOST, 3 * hidden_width)
    spread = spread[(inverse ^ shift).reshape(expert_peers, home_slots)]
    spread = lax.all_to_all(spread, "expert", split_axis=0, concat_axis=0, tiled=True)
    mine_rows = jnp.transpose(spread, (1, 0, 2, 3)).reshape(
        home_slots, cell_count, 3 * hidden_width
    )

    outs, row_grads = [], []
    for part_payload, (gu_pieces, dn_pieces) in zip(payloads, pieces):
        outs.append(
            jnp.concatenate(
                [
                    jnp.einsum(
                        "hrf,hfd->hrd",
                        part_payload[..., 2 * hidden_width :],
                        piece,
                        preferred_element_type=jnp.float32,
                    ).astype(jnp.bfloat16)
                    for piece in dn_pieces
                ],
                axis=-1,
            )
        )
        row_grads.append(
            jnp.concatenate(
                [
                    jnp.einsum(
                        "hrf,hdf->hrd",
                        part_payload[..., : 2 * hidden_width],
                        piece,
                        preferred_element_type=jnp.float32,
                    ).astype(jnp.bfloat16)
                    for piece in gu_pieces
                ],
                axis=-1,
            )
        )
    expert_out = jnp.concatenate(outs, axis=0)
    d_rows = jnp.concatenate(row_grads, axis=0)
    cells = (home_slots, expert_peers, MOST, model_width)
    scaled_out = cell_gate[..., None] * expert_out.reshape(cells).astype(jnp.float32)
    part_out = jnp.einsum(
        "shmt,hsmd->std",
        select.astype(jnp.float32),
        scaled_out,
        precision=lax.Precision.HIGHEST,
        preferred_element_type=jnp.float32,
    ).astype(jnp.bfloat16)
    part_grad = pick_rows("shmt,hsmd->std", select, d_rows.reshape(cells)).astype(jnp.bfloat16)
    sent = jnp.concatenate([part_out, part_grad], axis=-1)
    sent, mine_rows = lax.optimization_barrier((sent, mine_rows))
    back = lax.all_to_all(
        sent,
        "expert",
        split_axis=0,
        concat_axis=0,
        tiled=True,
    )
    summed = jnp.sum(back.astype(jnp.float32), axis=0).astype(jnp.bfloat16)
    layer_out = swap_pieces(summed[:, :model_width], dp_peers, dp_index)
    d_tokens = swap_pieces(summed[:, model_width:], dp_peers, dp_index)

    group_payload = lax.all_gather(mine_rows, "dp", axis=1, tiled=True)
    grad_gu = jnp.einsum(
        "hrc,hrf->hcf",
        new_tokens,
        group_payload[..., : 2 * hidden_width],
        preferred_element_type=jnp.float32,
    ).astype(jnp.bfloat16)
    grad_dn = jnp.einsum(
        "hrf,hrc->hfc",
        group_payload[..., 2 * hidden_width :],
        new_douts,
        preferred_element_type=jnp.float32,
    ).astype(jnp.bfloat16)
    return (layer_out, d_tokens, grad_gu, grad_dn)


def shards(tokens, expert_ids, gate_values, w_gate_up, *rest):
    few_owners = lax.axis_size("expert") < expert_ids.shape[1]
    pairs = lax.axis_size("groups") == 2 and lax.axis_size("dp") == 4
    half = w_gate_up.shape[0] // (2 * PARTS)
    even = w_gate_up.shape[0] == 2 * PARTS * half and half > 0 and half & (half - 1) == 0
    body = shared_shards if few_owners and pairs and even else routed_shards
    return body(tokens, expert_ids, gate_values, w_gate_up, *rest)


def solution(mesh):
    return jax.shard_map(
        shards,
        mesh=mesh,
        in_specs=(
            P(("groups", "expert", "dp"), None),
            P(("groups", "expert", "dp"), None),
            P(("groups", "expert", "dp"), None),
            P("expert", "dp", None),
            P("expert", None, "dp"),
            P(),
            P(("groups", "expert", "dp"), None),
        ),
        out_specs=(
            P(("groups", "expert", "dp"), None),
            P(("groups", "expert", "dp"), None),
            P(("groups", "expert"), "dp", None),
            P(("groups", "expert"), None, "dp"),
        ),
        check_vma=False,
    )
```
